32 devices in a mesh: row: 4 (over x, core), col: 8 (over z, y).
Axes of the slice: x: 2, y: 2, z: 4, core: 2. Of those that a mesh axis runs over, the one named last changes fastest.
Arguments:
- basis: bfloat16 [576, 256, 128], P(('row', 'col')), may hold values from -1.5 to 1.5
- row_index: int32 [576, 128], P(('row', 'col')), may hold values from 0 to 255
- group_slot: int32 [576], P(('row', 'col')), may hold values from 0 to 767, as said below
- x_blocks: bfloat16 [48, 256, 256], P('row', 'col')
- zinv_blocks: bfloat16 [48, 256, 256], P('row', 'col')
Outputs:
- schur_tiles: float32 [48, 2048, 2048], P('row', None, 'col')
The draws below stay inside these ranges and needn't reach their ends.
Inputs may be any that keep to these rules, and one draw needn't show every extreme that they name: Values are distinct; group_slot // 16 is the group's PSD block and group_slot % 16 its position there. A group stored on the device at (row index a, col index c) has its position among c * 2 to c * 2 + 1. Of the groups of one device, at most 5 belong to blocks of one index of row (blocks b with b // 12 equal to it), and every device reaches 5 for some index. The positions that the blocks of one index of row have on one index of col hold exactly 18 groups.
All inputs are finite; a program needn't handle non-finite values.
Results may differ from the reference program's by a relative error of at most 0.00048.
Values may be sent and summed in bfloat16 or wider, within the bound.
No kernel may reach another device: no remote copies, remote signals or barrier semaphores. Data moves between devices by JAX's collectives and lax.ppermute only.
A program may use at most 192 MiB of HBM per device.

```python
import math
import jax
import jax.numpy as jnp
from jax import lax

N = 256
C = 128
GMAX = 16
BLK_ROW = 12
POS_DEV = 2
GRP_DEV = 18
NBLK = 48
NGRP = 576
N_ROW = 4
N_COL = 8


def definite_blocks(key):
    key_off, key_lift = jax.random.split(key)
    spread = jax.random.uniform(key_off, (NBLK, N, N), jnp.float32, -4.0 / N, 4.0 / N)
    lift = jnp.exp(jax.random.uniform(key_lift, (NBLK, N), jnp.float32, math.log(0.5), math.log(2.0)))
    identity = jnp.eye(N, dtype=jnp.float32)
    spread = 0.5 * (spread + jnp.swapaxes(spread, 1, 2))
    spread = spread * (1.0 - identity)
    diagonal = jnp.sum(jnp.abs(spread), axis=2) + lift
    return (spread + diagonal[:, :, None] * identity).astype(jnp.bfloat16)


def draw_x_blocks(key, part):
    return definite_blocks(jax.random.fold_in(key, 11))


def draw_zinv_blocks(key, part):
    return definite_blocks(jax.random.fold_in(key, 23))


def permute_count(one_key, count):
    order = jax.random.permutation(one_key, count).astype(jnp.int32)
    serial = jnp.arange(count, dtype=jnp.int32)
    score = jnp.where(order == count - 1, -2, jnp.where(order == 0, -1, serial))
    return order[jnp.argsort(score, stable=True)]


def draw_group_slot(key, part):
    places = BLK_ROW * POS_DEV
    key_recv, key_home = jax.random.split(jax.random.fold_in(key, 7))
    recv_keys = jax.random.split(key_recv, N_ROW * N_COL)
    recv_perm = jax.vmap(lambda one_key: permute_count(one_key, places))(recv_keys).reshape(N_ROW, N_COL, places).astype(jnp.int32)
    home_keys = jax.random.split(key_home, N_ROW * N_COL)
    home_perm = jax.vmap(lambda one_key: jax.random.permutation(one_key, GRP_DEV))(home_keys).reshape(N_ROW, N_COL, GRP_DEV).astype(jnp.int32)
    home_row = jnp.arange(N_ROW, dtype=jnp.int32)
    offset = (home_row[:, None] - home_row[None, :]) % N_ROW
    counts = (GRP_DEV - offset + N_ROW - 1) // N_ROW
    before = jnp.cumsum(counts, axis=1) - counts
    serial = jnp.arange(GRP_DEV, dtype=jnp.int32)
    owner_at = (home_row[:, None] + serial[None, :]) % N_ROW
    rounds = serial // N_ROW
    arrival = before[owner_at, home_row[:, None]] + rounds[None, :]
    col_ids = jnp.arange(N_COL, dtype=jnp.int32)
    local_spot = recv_perm[owner_at[:, None, :], col_ids[None, :, None], arrival[:, None, :]]
    block_id = owner_at[:, None, :] * BLK_ROW + local_spot // POS_DEV
    position = col_ids[None, :, None] * POS_DEV + local_spot % POS_DEV
    slot_id = block_id * GMAX + position
    ordered = jnp.take_along_axis(slot_id, home_perm, axis=2)
    return ordered.reshape(-1).astype(jnp.int32)


def touch_ends(result, stream_key, least, largest):
    index_at = [jax.random.randint(jax.random.fold_in(stream_key, axis), (), 0, length) for axis, length in enumerate(result.shape)]
    longest = result.shape.index(max(result.shape))
    next_to = index_at[:longest] + [(index_at[longest] + 1) % result.shape[longest]] + index_at[longest + 1:]
    return result.at[tuple(index_at)].set(least).at[tuple(next_to)].set(largest)


def steps_of(rng, extent, cuts, least, top_value):
    def one(axis_at, blocks):
        steps = jax.random.uniform(jax.random.fold_in(jax.random.fold_in(rng, 6), axis_at), (blocks,), jnp.float32, least / len(cuts), top_value / len(cuts))
        return jnp.repeat(jnp.exp(steps), extent[axis_at] // blocks).reshape((-1,) + (1,) * (len(extent) - axis_at - 1))

    loudness = one(*cuts[0])
    for cut in cuts[1:]:
        loudness = loudness * one(*cut)
    return loudness


def gaussian(key, dims, scale, reach, pieces=(), kind=jnp.bfloat16):
    values = jax.random.normal(key, dims, jnp.float32) * scale
    if len(pieces) > 0:
        values = steps_of(key, dims, pieces, -0.22, 0.18) * values
    return jnp.clip(values, min=-reach, max=reach).astype(kind)


def setup_inputs(seed: int = 0) -> dict:
    key_of = jax.random.split(jax.random.key(seed), 6)
    return {
        "basis": gaussian(key_of[0], (NGRP, N, C), 0.25, 1.5, ((0, 32),)),
        "row_index": touch_ends(jax.random.randint(key_of[1], (NGRP, C), 0, N), jax.random.fold_in(key_of[1], 1), 0, N - 1).astype(jnp.int32),
        "group_slot": draw_group_slot(jax.random.fold_in(key_of[5], 71), 0),
        "x_blocks": draw_x_blocks(jax.random.fold_in(key_of[5], 71), 0),
        "zinv_blocks": draw_zinv_blocks(jax.random.fold_in(key_of[5], 71), 0),
    }


def tile_block(members):
    basis_block, rows_block, mask_block, x_block, z_block = members
    basis_wide = basis_block.astype(jnp.float32)
    image_x = jnp.einsum("pnc,nm->pcm", basis_wide, x_block.astype(jnp.float32), precision=lax.Precision.HIGHEST).astype(jnp.bfloat16)
    image_z = jnp.einsum("pnc,nm->pcm", basis_wide, z_block.astype(jnp.float32), precision=lax.Precision.HIGHEST).astype(jnp.bfloat16)
    x_rows = jnp.take(x_block, rows_block, axis=0)
    z_rows = jnp.take(z_block, rows_block, axis=0)
    stacked = jnp.concatenate([image_x, x_rows, image_z, z_rows], axis=1)
    products = jnp.einsum("pcn,qnk->pcqk", stacked.astype(jnp.float32), basis_wide, precision=lax.Precision.HIGHEST)
    products = products.reshape(GMAX, 4 * C, GMAX * C)
    picked = jnp.take(stacked, rows_block.reshape(-1), axis=2).astype(jnp.float32)
    tile_sum = products[:, C:2 * C] * picked[:, 2 * C:3 * C] + picked[:, C:2 * C] * products[:, 2 * C:3 * C]
    tile_sum = tile_sum + products[:, :C] * picked[:, 3 * C:] + picked[:, :C] * products[:, 3 * C:]
    column_mask = jnp.repeat(mask_block, C)
    tile_sum = tile_sum * mask_block[:, None, None] * column_mask[None, None, :]
    return tile_sum.reshape(GMAX * C, GMAX * C)


def reference(basis, row_index, group_slot, x_blocks, zinv_blocks):
    slot_total = NBLK * GMAX
    placed = jnp.zeros((slot_total, N, C), jnp.bfloat16).at[group_slot].set(basis).reshape(NBLK, GMAX, N, C)
    placed_rows = jnp.zeros((slot_total, C), jnp.int32).at[group_slot].set(row_index).reshape(NBLK, GMAX, C)
    present = jnp.zeros((slot_total,), jnp.float32).at[group_slot].set(1.0).reshape(NBLK, GMAX)
    return lax.map(tile_block, (placed, placed_rows, present, x_blocks, zinv_blocks))
```

```python
import functools
import math

import jax
import jax.numpy as jnp
from jax import lax
from jax.experimental import pallas as pl
from jax.experimental.pallas import tpu as pltpu
from jax.sharding import PartitionSpec as P

GMAX = 16
LANES = 128
VMEM_LIMIT = 32 * 1024 * 1024
UNROLL = 3


def round_up(value, unit):
    return (value + unit - 1) // unit * unit


def ring_order(count):
    inner = max(d for d in range(1, math.isqrt(count) + 1) if count % d == 0)
    outer = count // inner
    path = []
    for line in range(outer):
        places = range(1, inner) if line % 2 == 0 else range(inner - 1, 0, -1)
        path += [line * inner + place for place in places]
    return path + [line * inner for line in range(outer - 1, -1, -1)]


def dot(left, right):
    return jnp.dot(left, right, preferred_element_type=jnp.float32)


def cost(groups, order, width, near, extra_bytes=0):
    steps = groups * width * order * (4 * order + 8 * near)
    moved = groups * width * (2 * order + 4 * near) + extra_bytes
    return pl.CostEstimate(flops=2 * steps, bytes_accessed=moved, transcendentals=0)


def whole(space=pltpu.VMEM):
    return pl.BlockSpec(memory_space=space)


def pack_kernel(dims, slot_ref, rows_ref, basis_ref, *refs):
    row_count, capacity, owned = dims
    outs = refs[:row_count]
    bins, notes, facts, counts, sems = refs[row_count:]
    groups, order, width = basis_ref.shape
    my_row = lax.axis_index("row")
    notes[...] = jnp.zeros_like(notes)
    facts[...] = jnp.zeros_like(facts)
    for shift in range(row_count):
        counts[shift] = 0
    lane = lax.broadcasted_iota(jnp.int32, (1, LANES), 1)

    def place(g, carry):
        slot = slot_ref[g]
        block = slot // GMAX
        owner = block // owned
        shift = lax.rem(owner - my_row + row_count, row_count)
        at = counts[shift]
        counts[shift] = at + 1
        start = pl.multiple_of(at * width, width)
        bins[shift, pl.ds(start, width), :] = basis_ref[g].T
        notes[shift, pl.ds(at, 1), :] = rows_ref[pl.ds(g, 1), :].astype(jnp.float32)
        fact = jnp.where(lane == 0, block - owner * owned + 1, 0)
        fact = jnp.where(lane == 1, slot - block * GMAX, fact)
        facts[shift, pl.ds(at, 1), :] = fact.astype(jnp.float32)
        return carry

    lax.fori_loop(0, groups, place, 0)
    copies = []
    for shift in range(row_count):
        bins[shift, capacity * width :, :width] = notes[shift].astype(jnp.bfloat16)
        bins[shift, capacity * width :, width : width + LANES] = facts[shift].astype(jnp.bfloat16)
        copies.append(pltpu.make_async_copy(bins.at[shift], outs[shift], sems.at[shift]))
        copies[-1].start()
    for copy in copies:
        copy.wait()


def pack(slots, rows, basis, row_count, capacity, owned):
    groups, order, width = basis.shape
    note_rows = round_up(capacity, 16)
    shape = (capacity * width + note_rows, order)
    return pl.pallas_call(
        functools.partial(pack_kernel, (row_count, capacity, owned)),
        out_shape=[jax.ShapeDtypeStruct(shape, jnp.bfloat16)] * row_count,
        in_specs=[whole(pltpu.SMEM), whole(), whole()],
        out_specs=[whole(pl.ANY)] * row_count,
        scratch_shapes=[
            pltpu.VMEM((row_count,) + shape, jnp.bfloat16),
            pltpu.VMEM((row_count, note_rows, width), jnp.float32),
            pltpu.VMEM((row_count, note_rows, LANES), jnp.float32),
            pltpu.SMEM((row_count,), jnp.int32),
            pltpu.SemaphoreType.DMA((row_count,)),
        ],
        compiler_params=pltpu.CompilerParams(vmem_limit_bytes=VMEM_LIMIT),
        name="pack",
    )(slots, rows, basis)


def compact_kernel(dims, *refs):
    row_count, capacity, groups, width, half, note_rows = dims
    bins = refs[:row_count]
    out, notes_in, notes, facts_in, facts, numbers, scalars, counts, sem = refs[row_count:]
    my_col = lax.axis_index("col")
    tail = capacity * width
    for shift in range(row_count):
        notes_in[shift] = bins[shift][tail:, :width].astype(jnp.float32)
        facts_in[shift] = bins[shift][tail:, width : width + LANES].astype(jnp.float32)
        numbers[shift] = facts_in[shift].astype(jnp.int32)
    copy = pltpu.make_async_copy(numbers, scalars, sem)
    copy.start()
    notes[...] = jnp.zeros_like(notes)
    facts[...] = jnp.zeros_like(facts)
    counts[0] = 0
    copy.wait()
    for shift in range(row_count):
        for k in range(capacity):

            @pl.when(scalars[shift, k, 0] > 0)
            def _():
                at = counts[0]
                counts[0] = at + 1
                start = at * width + jnp.where(at >= half, note_rows, 0)
                start = pl.multiple_of(start, 16)
                out[pl.ds(start, width), :] = bins[shift][k * width : (k + 1) * width, :]
                notes[pl.ds(at, 1), :] = notes_in[shift, k : k + 1, :]
                facts[pl.ds(at, 1), :] = facts_in[shift, k : k + 1, :]

    lane = lax.broadcasted_iota(jnp.int32, facts.shape, 1)
    marked = jnp.where(lane == 2, my_col.astype(jnp.float32), facts[...])
    middle = half * width
    out[middle : middle + note_rows, :width] = notes[...].astype(jnp.bfloat16)
    out[middle : middle + note_rows, width : width + LANES] = marked.astype(jnp.bfloat16)


def compact(bins, capacity, groups, width, half, note_rows):
    row_count = len(bins)
    order = bins[0].shape[1]
    bin_notes = bins[0].shape[0] - capacity * width
    return pl.pallas_call(
        functools.partial(compact_kernel, (row_count, capacity, groups, width, half, note_rows)),
        out_shape=jax.ShapeDtypeStruct((groups * width + note_rows, order), jnp.bfloat16),
        in_specs=[whole()] * row_count,
        out_specs=whole(),
        scratch_shapes=[
            pltpu.VMEM((row_count, bin_notes, width), jnp.float32),
            pltpu.VMEM((note_rows, width), jnp.float32),
            pltpu.VMEM((row_count, bin_notes, LANES), jnp.float32),
            pltpu.VMEM((note_rows, LANES), jnp.float32),
            pltpu.VMEM((row_count, bin_notes, LANES), jnp.int32),
            pltpu.SMEM((row_count, bin_notes, LANES), jnp.int32),
            pltpu.SMEM((1,), jnp.int32),
            pltpu.SemaphoreType.DMA,
        ],
        compiler_params=pltpu.CompilerParams(vmem_limit_bytes=VMEM_LIMIT),
        name="compact",
    )(*bins)


def read_notes(piece, start, note_rows, notes, facts, scalars, sem):
    width = notes.shape[1]
    notes[...] = piece[start : start + note_rows, :width].astype(jnp.float32)
    numbers = piece[start : start + note_rows, width : width + LANES].astype(jnp.float32)
    facts[...] = numbers.astype(jnp.int32)
    copy = pltpu.make_async_copy(facts, scalars, sem)
    copy.start()
    copy.wait()


def tiles_of(spans, dims, piece, notes, scalars, weights, out, stage, stage_sems):
    places, width = dims
    x_ref, z_ref, near_ref, pick_ref = weights
    order = x_ref.shape[1]
    slots = stage.shape[0]
    lane = lax.broadcasted_iota(jnp.int32, (width, order), 1).astype(jnp.float32)
    repeats = order // width

    def send(b, p, slot):
        start = pl.multiple_of(p * width, width)
        return pltpu.make_async_copy(
            stage.at[slot], out.at[b, pl.ds(start, width), :], stage_sems.at[slot]
        )

    def one(g, start, slot):
        b = scalars[g, 0] - 1
        p = scalars[g, 1]
        vectors = piece[pl.ds(start, width), :]
        turned = jnp.broadcast_to(notes[pl.ds(g, 1), :], (width, width)).T
        row_pick = (jnp.concatenate([turned] * repeats, axis=1) == lane).astype(jnp.bfloat16)
        left = jnp.concatenate([vectors, row_pick], axis=0)
        x_half = dot(left, x_ref[b]).astype(jnp.bfloat16)
        z_half = dot(left, z_ref[b]).astype(jnp.bfloat16)
        near, pick = near_ref[b], pick_ref[b]
        su_x, se_x = dot(x_half, near), dot(x_half, pick)
        su_z, se_z = dot(z_half, near), dot(z_half, pick)
        tile = su_x[width:] * se_z[:width] + se_x[width:] * su_z[:width]
        tile = tile + (su_x[:width] * se_z[width:] + se_x[:width] * su_z[width:])
        stage[slot] = tile
        send(b, p, slot).start()

    unroll = slots // 2
    rounds = 0
    for first, count, base in spans:
        whole_rounds = count // unroll

        def body(i, carry, first=first, base=base, rounds=rounds):
            bank = lax.rem(rounds + i, 2) * unroll

            @pl.when(rounds + i >= 2)
            def _():
                for k in range(unroll):
                    send(0, 0, bank + k).wait()

            for k in range(unroll):
                start = pl.multiple_of(base + (i * unroll + k) * width, 16)
                one(first + i * unroll + k, start, bank + k)
            return carry

        lax.fori_loop(0, whole_rounds, body, 0)
        rounds += whole_rounds
        rest = count - whole_rounds * unroll
        if rest:
            bank = rounds % 2 * unroll
            if rounds >= 2:
                for k in range(unroll):
                    send(0, 0, bank + k).wait()
            for k in range(rest):
                at = whole_rounds * unroll + k
                one(first + at, base + at * width, bank + k)
            for k in range(rest):
                send(0, 0, bank + k).wait()
            if rounds >= 1:
                for k in range(unroll):
                    send(0, 0, (unroll - bank) + k).wait()
            rounds = 0
    for last in range(max(rounds - 2, 0), rounds):
        for k in range(unroll):
            send(0, 0, last % 2 * unroll + k).wait()


def blank_tiles(groups, dims, scalars, flags, blank, out, sems):
    places, width = dims
    owned = out.shape[0]
    spots = owned * places

    def clear(s, carry):
        flags[s] = 0
        return carry

    def mark(g, carry):
        spot = (scalars[g, 0] - 1) * places + scalars[g, 1] - scalars[0, 2] * places
        flags[spot] = 1
        return carry

    def copy(s):
        b = s // places
        start = pl.multiple_of((scalars[0, 2] * places + s - b * places) * width, width)
        return pltpu.make_async_copy(blank, out.at[b, pl.ds(start, width), :], sems.at[s])

    def start(s, carry):
        @pl.when(flags[s] == 0)
        def _():
            copy(s).start()

        return carry

    def wait(s, carry):
        @pl.when(flags[s] == 0)
        def _():
            copy(s).wait()

        return carry

    lax.fori_loop(0, spots, clear, 0)
    lax.fori_loop(0, groups, mark, 0)
    lax.fori_loop(0, spots, start, 0)
    return lambda: lax.fori_loop(0, spots, wait, 0)


def first_kernel(dims, tables, *refs):
    groups, places, width, half, note_rows, parts, part = dims
    x_parts, z_parts = refs[:parts], refs[parts : 2 * parts]
    refs = refs[2 * parts :]
    piece, x_ref, z_ref, near_ref, pick_ref, out = refs[:6]
    notes, facts, scalars, near_rows, stage, blank = refs[6:12]
    flags, part_sems, note_sem, stage_sems, blank_sems = refs[12:]
    my_col = lax.axis_index("col")
    owned, order = x_ref.shape[:2]
    copies = []
    for side, (sources, ref, table) in enumerate(
        ((x_parts, x_ref, tables[0]), (z_parts, z_ref, tables[1]))
    ):
        for k in range(parts):
            col = jnp.int32(0)
            for c in range(parts):
                col = jnp.where(my_col == c, jnp.int32(table[c][k]), col)
            start = pl.multiple_of(col * part, part)
            copies.append(
                pltpu.make_async_copy(
                    sources[k], ref.at[:, pl.ds(start, part), :], part_sems.at[side * parts + k]
                )
            )
            copies[-1].start()
    blank[...] = jnp.zeros_like(blank)
    near_ref[...] = jnp.zeros_like(near_ref)
    near_rows[...] = jnp.full(near_rows.shape, -1.0, jnp.float32)
    read_notes(piece, half * width, note_rows, notes, facts, scalars, note_sem)
    blanks_done = blank_tiles(groups, (places, width), scalars, flags, blank, out, blank_sems)

    def settle(g, carry):
        b = scalars[g, 0] - 1
        place = scalars[g, 1] - my_col * places
        start = pl.multiple_of(g * width + jnp.where(g >= half, note_rows, 0), 16)
        turned = piece[pl.ds(start, width), :].T
        for k in range(places):

            @pl.when(place == k)
            def _():
                near_ref[b, :, k * width : (k + 1) * width] = turned
                near_rows[b, k : k + 1, :] = notes[pl.ds(g, 1), :]

        return carry

    lax.fori_loop(0, groups, settle, 0)
    deep = lax.broadcasted_iota(jnp.int32, (order, width), 0).astype(jnp.float32)

    def picks(b, carry):
        for k in range(places):
            hit = near_rows[b, k : k + 1, :] == deep
            pick_ref[b, :, k * width : (k + 1) * width] = hit.astype(jnp.bfloat16)
        return carry

    lax.fori_loop(0, owned, picks, 0)
    for copy in copies:
        copy.wait()
    spans = [(0, half, 0), (half, groups - half, half * width + note_rows)]
    weights = (x_ref, z_ref, near_ref, pick_ref)
    tiles_of(spans, (places, width), piece, notes, scalars, weights, out, stage, stage_sems)
    blanks_done()


def first_tiles(x_parts, z_parts, own, tables, sizes):
    groups, places, width, half, note_rows = sizes
    parts = len(x_parts)
    owned, part, order = x_parts[0].shape
    near = places * width
    square = jax.ShapeDtypeStruct((owned, order, order), jnp.bfloat16)
    narrow = jax.ShapeDtypeStruct((owned, order, near), jnp.bfloat16)
    out = jax.ShapeDtypeStruct((owned, GMAX * width, near), jnp.float32)
    return pl.pallas_call(
        functools.partial(
            first_kernel, (groups, places, width, half, note_rows, parts, part), tables
        ),
        out_shape=[square, square, narrow, narrow, out],
        in_specs=[whole(pl.ANY)] * (2 * parts) + [whole()],
        out_specs=[whole()] * 4 + [whole(pl.ANY)],
        scratch_shapes=[
            pltpu.VMEM((note_rows, width), jnp.float32),
            pltpu.VMEM((note_rows, LANES), jnp.int32),
            pltpu.SMEM((note_rows, LANES), jnp.int32),
            pltpu.VMEM((owned, round_up(places, 8), width), jnp.float32),
            pltpu.VMEM((2 * UNROLL, width, near), jnp.float32),
            pltpu.VMEM((width, near), jnp.float32),
            pltpu.SMEM((owned * places,), jnp.int32),
            pltpu.SemaphoreType.DMA((2 * parts,)),
            pltpu.SemaphoreType.DMA,
            pltpu.SemaphoreType.DMA((2 * UNROLL,)),
            pltpu.SemaphoreType.DMA((owned * places,)),
        ],
        cost_estimate=cost(groups, order, width, near),
        compiler_params=pltpu.CompilerParams(vmem_limit_bytes=VMEM_LIMIT),
        name="first_tiles",
    )(*x_parts, *z_parts, own)


def next_kernel(dims, plans, *refs):
    groups, places, width, note_rows = dims
    count = len(plans)
    pieces, weights = refs[:count], refs[count : count + 4]
    out, notes, facts, scalars, stage, blank = refs[count + 5 : count + 11]
    flags, note_sem, stage_sems, blank_sems = refs[count + 11 :]
    blank[...] = jnp.zeros_like(blank)
    for k, (note_start, spans, fills) in enumerate(plans):
        read_notes(pieces[k], note_start, note_rows, notes, facts, scalars, note_sem)
        if fills:
            blanks_done = blank_tiles(
                groups, (places, width), scalars, flags, blank, out, blank_sems
            )
        tiles_of(
            spans, (places, width), pieces[k], notes, scalars, weights, out, stage, stage_sems
        )
        if fills:
            blanks_done()


def next_tiles(pieces, plans, weights, out, sizes):
    groups, places, width, half, note_rows = sizes
    owned = out.shape[0]
    order = weights[0].shape[1]
    near = out.shape[2]
    count = len(pieces)
    return pl.pallas_call(
        functools.partial(next_kernel, (groups, places, width, note_rows), plans),
        out_shape=jax.ShapeDtypeStruct(out.shape, out.dtype),
        in_specs=[whole()] * (count + 4) + [whole(pl.ANY)],
        out_specs=whole(pl.ANY),
        input_output_aliases={count + 4: 0},
        scratch_shapes=[
            pltpu.VMEM((note_rows, width), jnp.float32),
            pltpu.VMEM((note_rows, LANES), jnp.int32),
            pltpu.SMEM((note_rows, LANES), jnp.int32),
            pltpu.VMEM((2 * UNROLL, width, near), jnp.float32),
            pltpu.VMEM((width, near), jnp.float32),
            pltpu.SMEM((owned * places,), jnp.int32),
            pltpu.SemaphoreType.DMA,
            pltpu.SemaphoreType.DMA((2 * UNROLL,)),
            pltpu.SemaphoreType.DMA((owned * places,)),
        ],
        cost_estimate=cost(
            sum(span[1] for plan in plans for span in plan[1]), order, width, near
        ),
        compiler_params=pltpu.CompilerParams(vmem_limit_bytes=VMEM_LIMIT),
        name="next_tiles",
    )(*pieces, *weights, out)


def body(basis, row_index, group_slot, x_blocks, zinv_blocks):
    row_count = lax.axis_size("row")
    col_count = lax.axis_size("col")
    groups, order, width = basis.shape
    owned = x_blocks.shape[0]
    places = GMAX // col_count
    capacity = (groups + row_count - 1) // row_count
    half = groups // 2
    note_rows = round_up(groups, 16)
    sizes = (groups, places, width, half, note_rows)

    ring = ring_order(col_count)
    place_of = {col: k for k, col in enumerate(ring)}
    ahead = [(ring[k], ring[(k + 1) % col_count]) for k in range(col_count)]
    behind = [(there, here) for here, there in ahead]
    full_steps = (col_count - 1) // 2
    split = col_count % 2 == 0 and col_count > 1

    x_parts, z_parts = [x_blocks], [zinv_blocks]
    x_from, z_from = [0], [0]
    going = [[x_blocks, zinv_blocks], [x_blocks, zinv_blocks]]
    for step in range(1, full_steps + 1):
        for way, (pairs, sign) in enumerate(((ahead, -1), (behind, 1))):
            going[way] = [lax.ppermute(held, "col", pairs) for held in going[way]]
            x_parts.append(going[way][0])
            z_parts.append(going[way][1])
            x_from.append(sign * step)
            z_from.append(sign * step)
    if split:
        x_parts.append(lax.ppermute(going[0][0], "col", ahead))
        z_parts.append(lax.ppermute(going[1][1], "col", behind))
        x_from.append(-(full_steps + 1))
        z_from.append(full_steps + 1)

    def table(offsets):
        return [
            [ring[(place_of[col] + offset) % col_count] for offset in offsets]
            for col in range(col_count)
        ]

    bins = pack(group_slot, row_index, basis, row_count, capacity, owned)
    got = [bins[0]]
    for shift in range(1, row_count):
        pairs = [(k, (k + shift) % row_count) for k in range(row_count)]
        got.append(lax.ppermute(bins[shift], "row", pairs))
    own = compact(got, capacity, groups, width, half, note_rows)

    own, x_parts, z_parts = lax.optimization_barrier((own, x_parts, z_parts))
    *weights, out = first_tiles(x_parts, z_parts, own, (table(x_from), table(z_from)), sizes)

    middle = half * width
    both = [(0, half, 0), (half, groups - half, middle + note_rows)]
    going = [own, own]
    for step in range(1, full_steps + 1):
        arrived = [lax.ppermute(going[0], "col", ahead), lax.ppermute(going[1], "col", behind)]
        going, out = lax.optimization_barrier((arrived, out))
        plans = [(middle, both, True)] * 2
        out = next_tiles(going, plans, weights, out, sizes)
    if split:
        lower = lax.ppermute(going[0][: middle + note_rows], "col", ahead)
        upper = lax.ppermute(going[1][middle:], "col", behind)
        plans = [(middle, [(0, half, 0)], True), (0, [(half, groups - half, note_rows)], False)]
        out = next_tiles([lower, upper], plans, weights, out, sizes)
    return out


def solution(mesh):
    placed = (
        P(("row", "col"), None, None),
        P(("row", "col"), None),
        P(("row", "col")),
        P("row", "col", None),
        P("row", "col", None),
    )
    return jax.shard_map(
        body, mesh=mesh, in_specs=placed, out_specs=P("row", None, "col"), check_vma=False
    )
```

```python
import functools
import math

import jax
import jax.numpy as jnp
from jax import lax
from jax.experimental import pallas as pl
from jax.experimental.pallas import tpu as pltpu
from jax.sharding import PartitionSpec as P

GMAX = 16
LANES = 128
VMEM_LIMIT = 32 * 1024 * 1024
UNROLL = 5


def round_up(value, unit):
    return (value + unit - 1) // unit * unit


def ring_order(count):
    inner = max(d for d in range(1, math.isqrt(count) + 1) if count % d == 0)
    outer = count // inner
    path = []
    for line in range(outer):
        places = range(1, inner) if line % 2 == 0 else range(inner - 1, 0, -1)
        path += [line * inner + place for place in places]
    return path + [line * inner for line in range(outer - 1, -1, -1)]


def dot(left, right):
    return jnp.dot(left, right, preferred_element_type=jnp.float32)


def partner(place, turn, count):
    return place ^ turn if count & (count - 1) == 0 else (place + turn) % count


def side_by_side(counts):
    return max(k for k in range(1, UNROLL + 1) if all(count % k == 0 for count in counts))


def cost(groups, order, width, near, extra_bytes=0):
    steps = groups * width * order * (4 * order + 8 * near)
    moved = groups * width * (2 * order + 4 * near) + extra_bytes
    return pl.CostEstimate(flops=2 * steps, bytes_accessed=moved, transcendentals=0)


def whole(space=pltpu.VMEM):
    return pl.BlockSpec(memory_space=space)


def pack_kernel(dims, slot_ref, rows_ref, basis_ref, *refs):
    row_count, capacity, owned = dims
    outs = refs[:row_count]
    bins, notes, facts, counts, sems = refs[row_count:]
    groups, order, width = basis_ref.shape
    my_row = lax.axis_index("row")
    notes[...] = jnp.zeros_like(notes)
    facts[...] = jnp.zeros_like(facts)
    for shift in range(row_count):
        counts[shift] = 0
    lane = lax.broadcasted_iota(jnp.int32, (1, LANES), 1)

    def place(g, carry):
        slot = slot_ref[g]
        block = slot // GMAX
        owner = block // owned
        if row_count & (row_count - 1) == 0:
            shift = owner ^ my_row
        else:
            shift = lax.rem(owner - my_row + row_count, row_count)
        at = counts[shift]
        counts[shift] = at + 1
        start = pl.multiple_of(notes.shape[1] + at * width, 16)
        bins[shift, pl.ds(start, width), :] = basis_ref[g].T
        notes[shift, pl.ds(at, 1), :] = rows_ref[pl.ds(g, 1), :].astype(jnp.float32)
        fact = jnp.where(lane == 0, block - owner * owned + 1, 0)
        fact = jnp.where(lane == 1, slot - block * GMAX, fact)
        facts[shift, pl.ds(at, 1), :] = fact.astype(jnp.float32)
        return carry

    lax.fori_loop(0, groups, place, 0)
    copies = []
    for shift in range(row_count):
        bins[shift, : notes.shape[1], :width] = notes[shift].astype(jnp.bfloat16)
        bins[shift, : notes.shape[1], width : width + LANES] = facts[shift].astype(jnp.bfloat16)
        copies.append(pltpu.make_async_copy(bins.at[shift], outs[shift], sems.at[shift]))
        copies[-1].start()
    for copy in copies:
        copy.wait()


def pack(slots, rows, basis, row_count, capacity, owned):
    groups, order, width = basis.shape
    note_rows = round_up(capacity, 16)
    shape = (capacity * width + note_rows, order)
    return pl.pallas_call(
        functools.partial(pack_kernel, (row_count, capacity, owned)),
        out_shape=[jax.ShapeDtypeStruct(shape, jnp.bfloat16)] * row_count,
        in_specs=[whole(pltpu.SMEM), whole(), whole()],
        out_specs=[whole(pl.ANY)] * row_count,
        scratch_shapes=[
            pltpu.VMEM((row_count,) + shape, jnp.bfloat16),
            pltpu.VMEM((row_count, note_rows, width), jnp.float32),
            pltpu.VMEM((row_count, note_rows, LANES), jnp.float32),
            pltpu.SMEM((row_count,), jnp.int32),
            pltpu.SemaphoreType.DMA((row_count,)),
        ],
        compiler_params=pltpu.CompilerParams(vmem_limit_bytes=VMEM_LIMIT),
        name="pack",
    )(slots, rows, basis)


def compact_kernel(dims, *refs):
    capacity, width, skip, take, bin_notes, note_rows = dims
    bin_count = len(refs) - 9
    bins, out = refs[:bin_count], refs[bin_count]
    notes_in, notes, facts_in, facts, numbers, scalars, counts, sem = refs[bin_count + 1 :]
    for shift in range(bin_count):
        notes_in[shift] = bins[shift][:bin_notes, :width].astype(jnp.float32)
        facts_in[shift] = bins[shift][:bin_notes, width : width + LANES].astype(jnp.float32)
        numbers[shift] = facts_in[shift].astype(jnp.int32)
    copy = pltpu.make_async_copy(numbers, scalars, sem)
    copy.start()
    notes[...] = jnp.zeros_like(notes)
    facts[...] = jnp.zeros_like(facts)
    counts[0] = 0
    copy.wait()
    for shift in range(bin_count):
        for k in range(capacity):
            here = scalars[shift, k, 0] > 0
            seen = counts[0]
            counts[0] = seen + here.astype(jnp.int32)
            place = seen - skip

            @pl.when(here & (place >= 0) & (place < take))
            def _():
                notes[pl.ds(place, 1), :] = notes_in[shift, k : k + 1, :]
                facts[pl.ds(place, 1), :] = facts_in[shift, k : k + 1, :]
                start = pl.multiple_of(note_rows + place * width, 16)
                source = bin_notes + k * width
                out[pl.ds(start, width), :] = bins[shift][source : source + width, :]

    out[:note_rows, :width] = notes[...].astype(jnp.bfloat16)
    out[:note_rows, width : width + LANES] = facts[...].astype(jnp.bfloat16)


def compact(bins, capacity, width, skip, take, note_rows):
    bin_count = len(bins)
    order = bins[0].shape[1]
    bin_notes = bins[0].shape[0] - capacity * width
    dims = (capacity, width, skip, take, bin_notes, note_rows)
    return pl.pallas_call(
        functools.partial(compact_kernel, dims),
        out_shape=jax.ShapeDtypeStruct((note_rows + take * width, order), jnp.bfloat16),
        in_specs=[whole()] * bin_count,
        out_specs=whole(),
        scratch_shapes=[
            pltpu.VMEM((bin_count, bin_notes, width), jnp.float32),
            pltpu.VMEM((note_rows, width), jnp.float32),
            pltpu.VMEM((bin_count, bin_notes, LANES), jnp.float32),
            pltpu.VMEM((note_rows, LANES), jnp.float32),
            pltpu.VMEM((bin_count, bin_notes, LANES), jnp.int32),
            pltpu.SMEM((bin_count, bin_notes, LANES), jnp.int32),
            pltpu.SMEM((1,), jnp.int32),
            pltpu.SemaphoreType.DMA,
        ],
        compiler_params=pltpu.CompilerParams(vmem_limit_bytes=VMEM_LIMIT),
        name="compact",
    )(*bins)


def read_notes(pieces, notes, facts):
    note_rows = notes.shape[0] // len(pieces)
    width = notes.shape[1]
    for k, piece in enumerate(pieces):
        rows = slice(k * note_rows, (k + 1) * note_rows)
        notes[rows, :] = piece[:note_rows, :width].astype(jnp.float32)
        numbers = piece[:note_rows, width : width + LANES].astype(jnp.float32)
        facts[rows, :] = numbers.astype(jnp.int32)


def spot_of(facts, note):
    fact = facts[pl.ds(note, 1), :]
    return fact[0, 0] - 1, fact[0, 1]


def tiles_of(spans, width, notes, facts, weights, out, stage, stage_sems):
    x_ref, z_ref, near_ref, pick_ref = weights
    order = x_ref.shape[1]
    unroll = stage.shape[0] // 2
    lane = lax.broadcasted_iota(jnp.int32, (width, order), 1).astype(jnp.float32)
    repeats = order // width

    def send(b, p, slot):
        start = pl.multiple_of(p * width, width)
        return pltpu.make_async_copy(
            stage.at[slot], out.at[b, pl.ds(start, width), :], stage_sems.at[slot]
        )

    def images(piece, note, start):
        b, p = spot_of(facts, note)
        vectors = piece[pl.ds(start, width), :]
        turned = jnp.broadcast_to(notes[pl.ds(note, 1), :], (width, width)).T
        row_pick = (jnp.concatenate([turned] * repeats, axis=1) == lane).astype(jnp.bfloat16)
        left = jnp.concatenate([vectors, row_pick], axis=0)
        x_half = dot(left, x_ref[b]).astype(jnp.bfloat16)
        z_half = dot(left, z_ref[b]).astype(jnp.bfloat16)
        return b, p, jnp.concatenate([x_half, z_half], axis=0)

    def tile(b, p, halves, slot):
        su, se = dot(halves, near_ref[b]), dot(halves, pick_ref[b])
        su_yx, su_x, su_yz, su_z = (su[k * width : (k + 1) * width] for k in range(4))
        se_yx, se_x, se_yz, se_z = (se[k * width : (k + 1) * width] for k in range(4))
        stage[slot] = (su_x * se_yz + se_x * su_yz) + (su_yx * se_z + se_yx * su_z)
        send(b, p, slot).start()

    def side_by_side_tiles(piece, first, base, count, bank):
        found = [
            images(piece, first + k, pl.multiple_of(base + k * width, 16)) for k in range(count)
        ]
        for k, held in enumerate(found):
            tile(*held, bank * unroll + k)

    waiting = [0, 0]

    def drain(bank, count):
        for k in range(count):
            send(0, 0, bank * unroll + k).wait()

    rounds = 0
    for piece, base, first, count in spans:
        full, rest = divmod(count, unroll)
        if full > 2:
            for bank in range(2):
                drain(bank, waiting[bank])

            def body(i, carry, piece=piece, base=base, first=first):
                bank = lax.rem(i, 2)

                @pl.when(i >= 2)
                def _():
                    drain(bank, unroll)

                at = i * unroll
                side_by_side_tiles(piece, first + at, base + at * width, unroll, bank)
                return carry

            lax.fori_loop(0, full, body, 0)
            waiting[:] = [unroll, unroll]
            rounds = full
        sizes = [] if full > 2 else [unroll] * full
        done = full * unroll if full > 2 else 0
        for size in sizes + ([rest] if rest else []):
            bank = rounds % 2
            drain(bank, waiting[bank])
            side_by_side_tiles(piece, first + done, base + done * width, size, bank)
            waiting[bank] = size
            done += size
            rounds += 1
    for bank in range(2):
        drain(bank, waiting[bank])


def blank_kernel(blocks, *refs):
    out, blank, sems = refs[-3:]
    blank[...] = jnp.zeros_like(blank)
    deep_rows = blank.shape[0]
    per_block = out.shape[1] // deep_rows
    copies = []
    for b in blocks:
        for k in range(per_block):
            copies.append(
                pltpu.make_async_copy(
                    blank,
                    out.at[b, pl.ds(k * deep_rows, deep_rows), :],
                    sems.at[(b - blocks[0]) * per_block + k],
                )
            )
            copies[-1].start()
    for copy in copies:
        copy.wait()


def blank_tiles(shape, blocks, after, out=None):
    held = list(after) if out is None else [*after, out]
    deep_rows = shape[1] // 2
    return pl.pallas_call(
        functools.partial(blank_kernel, blocks),
        out_shape=jax.ShapeDtypeStruct(shape, jnp.float32),
        in_specs=[whole(pl.ANY)] * len(held),
        out_specs=whole(pl.ANY),
        input_output_aliases={} if out is None else {len(after): 0},
        scratch_shapes=[
            pltpu.VMEM((deep_rows, shape[2]), jnp.float32),
            pltpu.SemaphoreType.DMA((2 * len(blocks),)),
        ],
        cost_estimate=pl.CostEstimate(
            flops=0, bytes_accessed=4 * len(blocks) * shape[1] * shape[2], transcendentals=0
        ),
        compiler_params=pltpu.CompilerParams(vmem_limit_bytes=VMEM_LIMIT),
        name="blank_tiles",
    )(*held)


def settle_kernel(dims, *refs):
    counts, places, width, note_rows = dims
    pieces, (near_ref, pick_ref) = refs[:2], refs[2:4]
    notes, facts, near_rows = refs[4:]
    my_col = lax.axis_index("col")
    owned, order = near_ref.shape[:2]
    near_ref[...] = jnp.zeros_like(near_ref)
    near_rows[...] = jnp.full(near_rows.shape, -1.0, jnp.float32)
    read_notes(pieces, notes, facts)

    for piece, count, first in zip(pieces, counts, (0, note_rows)):

        def settle(g, carry, piece=piece, first=first):
            b, place = spot_of(facts, first + g)
            place = place - my_col * places
            start = pl.multiple_of(note_rows + g * width, 16)
            turned = piece[pl.ds(start, width), :].T
            for k in range(places):

                @pl.when(place == k)
                def _():
                    near_ref[b, :, k * width : (k + 1) * width] = turned
                    near_rows[b, k : k + 1, :] = notes[pl.ds(first + g, 1), :]

            return carry

        lax.fori_loop(0, count, settle, 0)
    deep = lax.broadcasted_iota(jnp.int32, (order, width), 0).astype(jnp.float32)

    def picks(b, carry):
        for k in range(places):
            hit = near_rows[b, k : k + 1, :] == deep
            pick_ref[b, :, k * width : (k + 1) * width] = hit.astype(jnp.bfloat16)
        return carry

    lax.fori_loop(0, owned, picks, 0)


def settle_own(pieces, owned, sizes):
    counts, places, width, note_rows = sizes
    order = pieces[0].shape[1]
    near = places * width
    narrow = jax.ShapeDtypeStruct((owned, order, near), jnp.bfloat16)
    return pl.pallas_call(
        functools.partial(settle_kernel, (counts, places, width, note_rows)),
        out_shape=[narrow, narrow],
        in_specs=[whole()] * 2,
        out_specs=[whole()] * 2,
        scratch_shapes=[
            pltpu.VMEM((2 * note_rows, width), jnp.float32),
            pltpu.VMEM((2 * note_rows, LANES), jnp.int32),
            pltpu.VMEM((owned, round_up(places, 8), width), jnp.float32),
        ],
        cost_estimate=pl.CostEstimate(
            flops=0, bytes_accessed=8 * owned * order * near, transcendentals=0
        ),
        compiler_params=pltpu.CompilerParams(vmem_limit_bytes=VMEM_LIMIT),
        name="settle_own",
    )(*pieces)


def first_kernel(dims, tables, *refs):
    counts, width, note_rows, parts, part = dims
    held = refs[:parts]
    refs = refs[parts:]
    pieces, near_ref, pick_ref, x_ref, z_ref, out = refs[:2], *refs[2:4], *refs[5:8]
    owned = x_ref.shape[0]
    notes, facts, stage, part_sems, stage_sems = refs[8:]
    my_col = lax.axis_index("col")
    copies = []
    for k, (sides, sources) in enumerate(tables):
        col = jnp.int32(0)
        for c, source in enumerate(sources):
            col = jnp.where(my_col == c, jnp.int32(source), col)
        start = pl.multiple_of(col * part, part)
        for at, side in enumerate(sides):
            copies.append(
                pltpu.make_async_copy(
                    held[k].at[pl.ds(at * owned, owned)],
                    (x_ref, z_ref)[side].at[:, pl.ds(start, part), :],
                    part_sems.at[2 * k + at],
                )
            )
            copies[-1].start()
    read_notes(pieces, notes, facts)
    for copy in copies:
        copy.wait()
    spans = [
        (piece, note_rows, first, count)
        for piece, count, first in zip(pieces, counts, (0, note_rows))
    ]
    weights = (x_ref, z_ref, near_ref, pick_ref)
    tiles_of(spans, width, notes, facts, weights, out, stage, stage_sems)


def first_tiles(held, pieces, near_weights, out, tables, sizes):
    counts, places, width, note_rows = sizes
    parts = len(held)
    owned = out.shape[0]
    part, order = held[0].shape[1:]
    near = places * width
    slots = 2 * side_by_side(counts)
    square = jax.ShapeDtypeStruct((owned, order, order), jnp.bfloat16)
    return pl.pallas_call(
        functools.partial(first_kernel, (counts, width, note_rows, parts, part), tables),
        out_shape=[square, square, jax.ShapeDtypeStruct(out.shape, out.dtype)],
        in_specs=[whole(pl.ANY)] * parts + [whole()] * 4 + [whole(pl.ANY)],
        out_specs=[whole()] * 2 + [whole(pl.ANY)],
        input_output_aliases={parts + 4: 2},
        scratch_shapes=[
            pltpu.VMEM((2 * note_rows, width), jnp.float32),
            pltpu.VMEM((2 * note_rows, LANES), jnp.int32),
            pltpu.VMEM((slots, width, near), jnp.float32),
            pltpu.SemaphoreType.DMA((2 * parts,)),
            pltpu.SemaphoreType.DMA((slots,)),
        ],
        cost_estimate=cost(sum(counts), order, width, near),
        compiler_params=pltpu.CompilerParams(vmem_limit_bytes=VMEM_LIMIT),
        name="first_tiles",
    )(*held, *pieces, *near_weights, out)


def next_kernel(spans, width, noted, count, *refs):
    pieces, weights = refs[:count], refs[count : count + 4]
    out, notes, facts, stage, stage_sems = refs[count + 5 :]
    read_notes(pieces[:noted], notes, facts)
    spans = [(pieces[k], base, first, groups) for k, base, first, groups in spans]
    tiles_of(spans, width, notes, facts, weights, out, stage, stage_sems)


def next_tiles(pieces, noted, spans, weights, out, sizes):
    counts, places, width, note_rows = sizes
    order = weights[0].shape[1]
    near = out.shape[2]
    count = len(pieces)
    slots = 2 * side_by_side([span[3] for span in spans])
    return pl.pallas_call(
        functools.partial(next_kernel, spans, width, noted, count),
        out_shape=jax.ShapeDtypeStruct(out.shape, out.dtype),
        in_specs=[whole()] * (count + 4) + [whole(pl.ANY)],
        out_specs=whole(pl.ANY),
        input_output_aliases={count + 4: 0},
        scratch_shapes=[
            pltpu.VMEM((noted * note_rows, width), jnp.float32),
            pltpu.VMEM((noted * note_rows, LANES), jnp.int32),
            pltpu.VMEM((slots, width, near), jnp.float32),
            pltpu.SemaphoreType.DMA((slots,)),
        ],
        cost_estimate=cost(sum(span[3] for span in spans), order, width, near),
        compiler_params=pltpu.CompilerParams(vmem_limit_bytes=VMEM_LIMIT),
        name="next_tiles",
    )(*pieces, *weights, out)


def body(basis, row_index, group_slot, x_blocks, zinv_blocks):
    row_count = lax.axis_size("row")
    col_count = lax.axis_size("col")
    groups, order, width = basis.shape
    owned = x_blocks.shape[0]
    places = GMAX // col_count
    capacity = (groups + row_count - 1) // row_count
    low = groups - (row_count - 2) * capacity
    early = 2 if 0 < low < groups else row_count
    low = low if early == 2 else groups // 2
    counts = (low, groups - low)
    note_rows = round_up(max(counts), 16)
    sizes = (counts, places, width, note_rows)

    ring = ring_order(col_count)
    place_of = {col: k for k, col in enumerate(ring)}
    ahead = [(ring[k], ring[(k + 1) % col_count]) for k in range(col_count)]
    behind = [(there, here) for here, there in ahead]
    full_steps = (col_count - 1) // 2
    split = col_count % 2 == 0 and col_count > 1

    def whose(offset):
        return [ring[(place_of[col] + offset) % col_count] for col in range(col_count)]

    bins = pack(group_slot, row_index, basis, row_count, capacity, owned)
    got = [bins[0]]
    for turn in range(1, row_count):
        pairs = [(k, partner(k, turn, row_count)) for k in range(row_count)]
        got.append(lax.ppermute(bins[turn], "row", pairs))
    own = [compact(got[:early], capacity, width, 0, counts[0], note_rows)]
    pairs_of = (ahead, behind)

    def both_ways(moving):
        return [lax.ppermute(moving[way], "col", pairs_of[way]) for way in range(2)]

    shape = (owned, GMAX * width, places * width)
    blocks = list(range(owned))
    parts = [jnp.concatenate([x_blocks, zinv_blocks], axis=0)]
    sides = [(0, 1)]
    held = list(parts)
    tables = [(side, whose(0)) for side in sides]
    going = [[part, part] for part in parts]
    out = None
    first = None
    for step in range(1, full_steps + 1):
        if step == 2:
            going, bins = lax.optimization_barrier((going, bins))
        if step == 3:
            going, got = lax.optimization_barrier((going, got))
        for k in range(len(parts)):
            going[k] = both_ways(going[k])
            for way, sign in enumerate((-1, 1)):
                held.append(going[k][way])
                tables.append((sides[k], whose(sign * step)))
        if step == 1:
            out = blank_tiles(shape, blocks[: owned // 2], going[-1])
        if step == max(full_steps - 1, 1):
            out = blank_tiles(shape, blocks[owned // 2 :], going[-1], out)
    if out is None:
        out = blank_tiles(shape, blocks, [])
    if full_steps:
        first = both_ways([own[0], own[0]])
        going, first, out = lax.optimization_barrier((going, first, out))
    if split:
        last = [going[0][0][:owned], going[0][1][owned:]]
        held += both_ways(last)
        tables += [((0,), whose(full_steps + 1)), ((1,), whose(full_steps + 1))]
    own.append(compact(got, capacity, width, counts[0], counts[1], note_rows))
    settled, _ = lax.optimization_barrier((own, going))
    near, pick = settle_own(settled, owned, sizes)

    streams = [[own[half], own[half]] for half in range(2)]
    arrived = []
    weights = None

    def advance(out, weights):
        if weights is None:
            x_full, z_full, out = first_tiles(held, own, (near, pick), out, tables, sizes)
            return out, (x_full, z_full, near, pick)
        pieces, noted, spans = arrived.pop(0)
        return next_tiles(pieces, noted, spans, weights, out, sizes), weights

    sent = 0
    for step in range(1, full_steps + 1):
        for half in range(2):
            moving = streams[half]
            if sent == 2:
                moving, near, pick = lax.optimization_barrier((moving, near, pick))
            if sent >= 3:
                if weights is None:
                    out, weights = advance(out, weights)
                out, weights = advance(out, weights)
                moving, out = lax.optimization_barrier((moving, out))
            moving = first if sent == 0 else both_ways(moving)
            streams[half] = moving
            spans = [(k, note_rows, k * note_rows, counts[half]) for k in range(2)]
            arrived.append((moving, 2, spans))
            sent += 1
    if split:
        for half in range(2):
            part = counts[half] // 2
            cut = note_rows + part * width
            moving = streams[half]
            if weights is None:
                out, weights = advance(out, weights)
            if arrived:
                out, weights = advance(out, weights)
                moving, out = lax.optimization_barrier((moving, out))
            moving = both_ways([moving[0][:cut], moving[1][cut:]])
            spans = [(0, note_rows, 0, part), (1, 0, part, counts[half] - part)]
            arrived.append((moving, 1, spans))
    if weights is None:
        out, weights = advance(out, weights)
    while arrived:
        out, weights = advance(out, weights)
    return out


def solution(mesh):
    placed = (
        P(("row", "col"), None, None),
        P(("row", "col"), None),
        P(("row", "col")),
        P("row", "col", None),
        P("row", "col", None),
    )
    return jax.shard_map(
        body, mesh=mesh, in_specs=placed, out_specs=P("row", None, "col"), check_vma=False
    )
```

```python
import functools
import math

import jax
import jax.numpy as jnp
from jax import lax
from jax.experimental import pallas as pl
from jax.experimental.pallas import tpu as pltpu
from jax.sharding import PartitionSpec as P

GMAX = 16
LANES = 128
VMEM_LIMIT = 32 * 1024 * 1024
PACK_LIMIT = 56 * 1024 * 1024
UNROLL = 5
KERNELS = (0, 0, 0, 1, 2, 4, 5, 6)


def round_up(value, unit):
    return (value + unit - 1) // unit * unit


def ring_order(count):
    inner = max(d for d in range(1, math.isqrt(count) + 1) if count % d == 0)
    outer = count // inner
    path = []
    for line in range(outer):
        places = range(1, inner) if line % 2 == 0 else range(inner - 1, 0, -1)
        path += [line * inner + place for place in places]
    return path + [line * inner for line in range(outer - 1, -1, -1)]


def dot(left, right):
    return jnp.dot(left, right, preferred_element_type=jnp.float32)


def partner(place, turn, count):
    return place ^ turn if count & (count - 1) == 0 else (place + turn) % count


def side_by_side(counts):
    return max(k for k in range(1, UNROLL + 1) if all(count % k == 0 for count in counts))


def cost(groups, order, width, near, extra_bytes=0):
    steps = groups * width * order * (4 * order + 8 * near)
    moved = groups * width * (2 * order + 4 * near) + extra_bytes
    return pl.CostEstimate(flops=2 * steps, bytes_accessed=moved, transcendentals=0)


def whole(space=pltpu.VMEM):
    return pl.BlockSpec(memory_space=space)


def pack_kernel(dims, slot_ref, rows_ref, basis_ref, *refs):
    row_count, capacity, owned = dims
    outs = refs[:row_count]
    held, notes, facts, counts, sems = refs[row_count:]
    groups, order, width = basis_ref.shape
    copies = [
        pltpu.make_async_copy(basis_ref.at[g], held.at[g], sems.at[g]) for g in range(groups)
    ]
    for copy in copies:
        copy.start()
    my_row = lax.axis_index("row")
    notes[...] = jnp.zeros_like(notes)
    facts[...] = jnp.zeros_like(facts)
    for shift in range(row_count):
        counts[shift] = 0
    note_rows = notes.shape[1]
    lane = lax.broadcasted_iota(jnp.int32, (1, LANES), 1)
    for g in range(groups):
        slot = slot_ref[g]
        block = slot // GMAX
        owner = block // owned
        if row_count & (row_count - 1) == 0:
            shift = owner ^ my_row
        else:
            shift = lax.rem(owner - my_row + row_count, row_count)
        at = counts[shift]
        counts[shift] = at + 1
        notes[shift, pl.ds(at, 1), :] = rows_ref[pl.ds(g, 1), :].astype(jnp.float32)
        fact = jnp.where(lane == 0, block - owner * owned + 1, 0)
        fact = jnp.where(lane == 1, slot - block * GMAX, fact)
        facts[shift, pl.ds(at, 1), :] = fact.astype(jnp.float32)
        copies[g].wait()
        turned = held[g].T
        start = pl.multiple_of(note_rows + at * width, 16)
        for k in range(row_count):

            @pl.when(shift == k)
            def _():
                outs[k][pl.ds(start, width), :] = turned

    for k in range(row_count):
        outs[k][:note_rows, :width] = notes[k].astype(jnp.bfloat16)
        outs[k][:note_rows, width : width + LANES] = facts[k].astype(jnp.bfloat16)


def pack(slots, rows, basis, row_count, capacity, owned):
    groups, order, width = basis.shape
    note_rows = round_up(capacity, 16)
    shape = (capacity * width + note_rows, order)
    return pl.pallas_call(
        functools.partial(pack_kernel, (row_count, capacity, owned)),
        out_shape=[jax.ShapeDtypeStruct(shape, jnp.bfloat16)] * row_count,
        in_specs=[whole(pltpu.SMEM), whole(), whole(pl.ANY)],
        out_specs=[whole()] * row_count,
        scratch_shapes=[
            pltpu.VMEM(basis.shape, jnp.bfloat16),
            pltpu.VMEM((row_count, note_rows, width), jnp.float32),
            pltpu.VMEM((row_count, note_rows, LANES), jnp.float32),
            pltpu.SMEM((row_count,), jnp.int32),
            pltpu.SemaphoreType.DMA((groups,)),
        ],
        compiler_params=pltpu.CompilerParams(vmem_limit_bytes=PACK_LIMIT),
        name="pack",
    )(slots, rows, basis)


def compact_kernel(dims, *refs):
    capacity, width, skip, take, bin_notes, note_rows = dims
    bin_count = len(refs) - 9
    bins, out = refs[:bin_count], refs[bin_count]
    notes_in, notes, facts_in, facts, numbers, scalars, counts, sem = refs[bin_count + 1 :]
    for shift in range(bin_count):
        notes_in[shift] = bins[shift][:bin_notes, :width].astype(jnp.float32)
        facts_in[shift] = bins[shift][:bin_notes, width : width + LANES].astype(jnp.float32)
        numbers[shift] = facts_in[shift].astype(jnp.int32)
    copy = pltpu.make_async_copy(numbers, scalars, sem)
    copy.start()
    notes[...] = jnp.zeros_like(notes)
    facts[...] = jnp.zeros_like(facts)
    counts[0] = 0
    copy.wait()
    for shift in range(bin_count):
        for k in range(capacity):
            here = scalars[shift, k, 0] > 0
            seen = counts[0]
            counts[0] = seen + here.astype(jnp.int32)
            place = seen - skip

            @pl.when(here & (place >= 0) & (place < take))
            def _():
                notes[pl.ds(place, 1), :] = notes_in[shift, k : k + 1, :]
                facts[pl.ds(place, 1), :] = facts_in[shift, k : k + 1, :]
                start = pl.multiple_of(note_rows + place * width, 16)
                source = bin_notes + k * width
                out[pl.ds(start, width), :] = bins[shift][source : source + width, :]

    out[:note_rows, :width] = notes[...].astype(jnp.bfloat16)
    out[:note_rows, width : width + LANES] = facts[...].astype(jnp.bfloat16)


def compact(bins, capacity, width, skip, take, note_rows):
    bin_count = len(bins)
    order = bins[0].shape[1]
    bin_notes = bins[0].shape[0] - capacity * width
    dims = (capacity, width, skip, take, bin_notes, note_rows)
    return pl.pallas_call(
        functools.partial(compact_kernel, dims),
        out_shape=jax.ShapeDtypeStruct((note_rows + take * width, order), jnp.bfloat16),
        in_specs=[whole()] * bin_count,
        out_specs=whole(),
        scratch_shapes=[
            pltpu.VMEM((bin_count, bin_notes, width), jnp.float32),
            pltpu.VMEM((note_rows, width), jnp.float32),
            pltpu.VMEM((bin_count, bin_notes, LANES), jnp.float32),
            pltpu.VMEM((note_rows, LANES), jnp.float32),
            pltpu.VMEM((bin_count, bin_notes, LANES), jnp.int32),
            pltpu.SMEM((bin_count, bin_notes, LANES), jnp.int32),
            pltpu.SMEM((1,), jnp.int32),
            pltpu.SemaphoreType.DMA,
        ],
        compiler_params=pltpu.CompilerParams(vmem_limit_bytes=VMEM_LIMIT),
        name="compact",
    )(*bins)


def read_notes(pieces, notes, facts):
    note_rows = notes.shape[0] // len(pieces)
    width = notes.shape[1]
    for k, piece in enumerate(pieces):
        rows = slice(k * note_rows, (k + 1) * note_rows)
        notes[rows, :] = piece[:note_rows, :width].astype(jnp.float32)
        numbers = piece[:note_rows, width : width + LANES].astype(jnp.float32)
        facts[rows, :] = numbers.astype(jnp.int32)


def spot_of(facts, note):
    fact = facts[pl.ds(note, 1), :]
    return fact[0, 0] - 1, fact[0, 1]


def tiles_of(spans, width, notes, facts, weights, out, stage, stage_sems):
    x_ref, z_ref, near_ref, pick_ref = weights
    order = x_ref.shape[1]
    unroll = stage.shape[0] // 2
    lane = lax.broadcasted_iota(jnp.int32, (width, order), 1).astype(jnp.float32)
    repeats = order // width

    def send(b, p, slot):
        start = pl.multiple_of(p * width, width)
        return pltpu.make_async_copy(
            stage.at[slot], out.at[b, pl.ds(start, width), :], stage_sems.at[slot]
        )

    def images(piece, note, start):
        b, p = spot_of(facts, note)
        vectors = piece[pl.ds(start, width), :]
        turned = jnp.broadcast_to(notes[pl.ds(note, 1), :], (width, width)).T
        row_pick = (jnp.concatenate([turned] * repeats, axis=1) == lane).astype(jnp.bfloat16)
        left = jnp.concatenate([vectors, row_pick], axis=0)
        x_half = dot(left, x_ref[b]).astype(jnp.bfloat16)
        z_half = dot(left, z_ref[b]).astype(jnp.bfloat16)
        return b, p, jnp.concatenate([x_half, z_half], axis=0)

    def tile(b, p, halves, slot):
        su, se = dot(halves, near_ref[b]), dot(halves, pick_ref[b])
        su_yx, su_x, su_yz, su_z = (su[k * width : (k + 1) * width] for k in range(4))
        se_yx, se_x, se_yz, se_z = (se[k * width : (k + 1) * width] for k in range(4))
        stage[slot] = (su_x * se_yz + se_x * su_yz) + (su_yx * se_z + se_yx * su_z)
        send(b, p, slot).start()

    def side_by_side_tiles(piece, first, base, count, bank):
        found = [
            images(piece, first + k, pl.multiple_of(base + k * width, 16)) for k in range(count)
        ]
        for k, held in enumerate(found):
            tile(*held, bank * unroll + k)

    waiting = [0, 0]

    def drain(bank, count):
        for k in range(count):
            send(0, 0, bank * unroll + k).wait()

    rounds = 0
    for piece, base, first, count in spans:
        full, rest = divmod(count, unroll)
        if full > 2:
            for bank in range(2):
                drain(bank, waiting[bank])

            def body(i, carry, piece=piece, base=base, first=first):
                bank = lax.rem(i, 2)

                @pl.when(i >= 2)
                def _():
                    drain(bank, unroll)

                at = i * unroll
                side_by_side_tiles(piece, first + at, base + at * width, unroll, bank)
                return carry

            lax.fori_loop(0, full, body, 0)
            waiting[:] = [unroll, unroll]
            rounds = full
        sizes = [] if full > 2 else [unroll] * full
        done = full * unroll if full > 2 else 0
        for size in sizes + ([rest] if rest else []):
            bank = rounds % 2
            drain(bank, waiting[bank])
            side_by_side_tiles(piece, first + done, base + done * width, size, bank)
            waiting[bank] = size
            done += size
            rounds += 1
    for bank in range(2):
        drain(bank, waiting[bank])


def blank_kernel(blocks, *refs):
    out, blank, sems = refs[-3:]
    blank[...] = jnp.zeros_like(blank)
    deep_rows = blank.shape[0]
    per_block = out.shape[1] // deep_rows
    copies = []
    for b in blocks:
        for k in range(per_block):
            copies.append(
                pltpu.make_async_copy(
                    blank,
                    out.at[b, pl.ds(k * deep_rows, deep_rows), :],
                    sems.at[(b - blocks[0]) * per_block + k],
                )
            )
            copies[-1].start()
    for copy in copies:
        copy.wait()


def blank_tiles(shape, blocks, after, out=None):
    held = list(after) if out is None else [*after, out]
    deep_rows = shape[1] // 2
    return pl.pallas_call(
        functools.partial(blank_kernel, blocks),
        out_shape=jax.ShapeDtypeStruct(shape, jnp.float32),
        in_specs=[whole(pl.ANY)] * len(held),
        out_specs=whole(pl.ANY),
        input_output_aliases={} if out is None else {len(after): 0},
        scratch_shapes=[
            pltpu.VMEM((deep_rows, shape[2]), jnp.float32),
            pltpu.SemaphoreType.DMA((2 * len(blocks),)),
        ],
        cost_estimate=pl.CostEstimate(
            flops=0, bytes_accessed=4 * len(blocks) * shape[1] * shape[2], transcendentals=0
        ),
        compiler_params=pltpu.CompilerParams(vmem_limit_bytes=VMEM_LIMIT),
        name="blank_tiles",
    )(*held)


def settle_kernel(dims, *refs):
    counts, places, width, note_rows = dims
    pieces, (near_ref, pick_ref) = refs[:2], refs[2:4]
    notes, facts, near_rows = refs[4:]
    my_col = lax.axis_index("col")
    owned, order = near_ref.shape[:2]
    near_ref[...] = jnp.zeros_like(near_ref)
    near_rows[...] = jnp.full(near_rows.shape, -1.0, jnp.float32)
    read_notes(pieces, notes, facts)

    for piece, count, first in zip(pieces, counts, (0, note_rows)):

        def settle(g, carry, piece=piece, first=first):
            b, place = spot_of(facts, first + g)
            place = place - my_col * places
            start = pl.multiple_of(note_rows + g * width, 16)
            turned = piece[pl.ds(start, width), :].T
            for k in range(places):

                @pl.when(place == k)
                def _():
                    near_ref[b, :, k * width : (k + 1) * width] = turned
                    near_rows[b, k : k + 1, :] = notes[pl.ds(first + g, 1), :]

            return carry

        lax.fori_loop(0, count, settle, 0)
    deep = lax.broadcasted_iota(jnp.int32, (order, width), 0).astype(jnp.float32)

    def picks(b, carry):
        for k in range(places):
            hit = near_rows[b, k : k + 1, :] == deep
            pick_ref[b, :, k * width : (k + 1) * width] = hit.astype(jnp.bfloat16)
        return carry

    lax.fori_loop(0, owned, picks, 0)


def settle_own(pieces, owned, sizes):
    counts, places, width, note_rows = sizes
    order = pieces[0].shape[1]
    near = places * width
    narrow = jax.ShapeDtypeStruct((owned, order, near), jnp.bfloat16)
    return pl.pallas_call(
        functools.partial(settle_kernel, (counts, places, width, note_rows)),
        out_shape=[narrow, narrow],
        in_specs=[whole()] * 2,
        out_specs=[whole()] * 2,
        scratch_shapes=[
            pltpu.VMEM((2 * note_rows, width), jnp.float32),
            pltpu.VMEM((2 * note_rows, LANES), jnp.int32),
            pltpu.VMEM((owned, round_up(places, 8), width), jnp.float32),
        ],
        cost_estimate=pl.CostEstimate(
            flops=0, bytes_accessed=8 * owned * order * near, transcendentals=0
        ),
        compiler_params=pltpu.CompilerParams(vmem_limit_bytes=VMEM_LIMIT),
        name="settle_own",
    )(*pieces)


def first_kernel(dims, tables, *refs):
    counts, width, note_rows, parts, part = dims
    held = refs[:parts]
    refs = refs[parts:]
    pieces, near_ref, pick_ref, x_ref, z_ref, out = refs[:2], *refs[2:4], *refs[5:8]
    owned = x_ref.shape[0]
    notes, facts, stage, part_sems, stage_sems = refs[8:]
    my_col = lax.axis_index("col")
    copies = []
    for k, (sides, sources) in enumerate(tables):
        col = jnp.int32(0)
        for c, source in enumerate(sources):
            col = jnp.where(my_col == c, jnp.int32(source), col)
        start = pl.multiple_of(col * part, part)
        for at, side in enumerate(sides):
            copies.append(
                pltpu.make_async_copy(
                    held[k].at[pl.ds(at * owned, owned)],
                    (x_ref, z_ref)[side].at[:, pl.ds(start, part), :],
                    part_sems.at[2 * k + at],
                )
            )
            copies[-1].start()
    read_notes(pieces, notes, facts)
    for copy in copies:
        copy.wait()
    spans = [
        (piece, note_rows, first, count)
        for piece, count, first in zip(pieces, counts, (0, note_rows))
    ]
    weights = (x_ref, z_ref, near_ref, pick_ref)
    tiles_of(spans, width, notes, facts, weights, out, stage, stage_sems)


def first_tiles(held, pieces, near_weights, out, tables, sizes):
    counts, places, width, note_rows = sizes
    parts = len(held)
    owned = out.shape[0]
    part, order = held[0].shape[1:]
    near = places * width
    slots = 2 * side_by_side(counts)
    square = jax.ShapeDtypeStruct((owned, order, order), jnp.bfloat16)
    return pl.pallas_call(
        functools.partial(first_kernel, (counts, width, note_rows, parts, part), tables),
        out_shape=[square, square, jax.ShapeDtypeStruct(out.shape, out.dtype)],
        in_specs=[whole(pl.ANY)] * parts + [whole()] * 4 + [whole(pl.ANY)],
        out_specs=[whole()] * 2 + [whole(pl.ANY)],
        input_output_aliases={parts + 4: 2},
        scratch_shapes=[
            pltpu.VMEM((2 * note_rows, width), jnp.float32),
            pltpu.VMEM((2 * note_rows, LANES), jnp.int32),
            pltpu.VMEM((slots, width, near), jnp.float32),
            pltpu.SemaphoreType.DMA((2 * parts,)),
            pltpu.SemaphoreType.DMA((slots,)),
        ],
        cost_estimate=cost(sum(counts), order, width, near),
        compiler_params=pltpu.CompilerParams(vmem_limit_bytes=VMEM_LIMIT),
        name="first_tiles",
    )(*held, *pieces, *near_weights, out)


def next_kernel(spans, width, noted, count, *refs):
    pieces, weights = refs[:count], refs[count : count + 4]
    out, notes, facts, stage, stage_sems = refs[count + 5 :]
    read_notes(pieces[:noted], notes, facts)
    spans = [(pieces[k], base, first, groups) for k, base, first, groups in spans]
    tiles_of(spans, width, notes, facts, weights, out, stage, stage_sems)


def next_tiles(pieces, noted, spans, weights, out, sizes):
    counts, places, width, note_rows = sizes
    order = weights[0].shape[1]
    near = out.shape[2]
    count = len(pieces)
    slots = 2 * side_by_side([span[3] for span in spans])
    return pl.pallas_call(
        functools.partial(next_kernel, spans, width, noted, count),
        out_shape=jax.ShapeDtypeStruct(out.shape, out.dtype),
        in_specs=[whole()] * (count + 4) + [whole(pl.ANY)],
        out_specs=whole(pl.ANY),
        input_output_aliases={count + 4: 0},
        scratch_shapes=[
            pltpu.VMEM((noted * note_rows, width), jnp.float32),
            pltpu.VMEM((noted * note_rows, LANES), jnp.int32),
            pltpu.VMEM((slots, width, near), jnp.float32),
            pltpu.SemaphoreType.DMA((slots,)),
        ],
        cost_estimate=cost(sum(span[3] for span in spans), order, width, near),
        compiler_params=pltpu.CompilerParams(vmem_limit_bytes=VMEM_LIMIT),
        name="next_tiles",
    )(*pieces, *weights, out)


def body(basis, row_index, group_slot, x_blocks, zinv_blocks):
    row_count = lax.axis_size("row")
    col_count = lax.axis_size("col")
    groups, order, width = basis.shape
    owned = x_blocks.shape[0]
    places = GMAX // col_count
    capacity = (groups + row_count - 1) // row_count
    low = groups - (row_count - 2) * capacity
    early = 2 if 0 < low < groups else row_count
    low = low if early == 2 else groups // 2
    counts = (low, groups - low)
    note_rows = round_up(max(counts), 16)
    sizes = (counts, places, width, note_rows)

    ring = ring_order(col_count)
    place_of = {col: k for k, col in enumerate(ring)}
    ahead = [(ring[k], ring[(k + 1) % col_count]) for k in range(col_count)]
    behind = [(there, here) for here, there in ahead]
    full_steps = (col_count - 1) // 2
    split = col_count % 2 == 0 and col_count > 1

    def whose(offset):
        return [ring[(place_of[col] + offset) % col_count] for col in range(col_count)]

    bins = pack(group_slot, row_index, basis, row_count, capacity, owned)
    got = [bins[0]]
    for turn in range(1, row_count):
        pairs = [(k, partner(k, turn, row_count)) for k in range(row_count)]
        got.append(lax.ppermute(bins[turn], "row", pairs))
    own = [compact(got[:early], capacity, width, 0, counts[0], note_rows)]
    pairs_of = (ahead, behind)

    def both_ways(moving):
        return [lax.ppermute(moving[way], "col", pairs_of[way]) for way in range(2)]

    shape = (owned, GMAX * width, places * width)
    blocks = list(range(owned))
    held, tables = [x_blocks, zinv_blocks], [((0,), whose(0)), ((1,), whose(0))]
    going = None
    out = None
    first = None
    for step in range(1, full_steps + 1):
        if step == 2:
            going, bins = lax.optimization_barrier((going, bins))
        if step == 3:
            going, got = lax.optimization_barrier((going, got))
        if step == 1:
            near_parts = [both_ways([part, part]) for part in (x_blocks, zinv_blocks)]
            near_parts = lax.optimization_barrier(near_parts)
            going = [jnp.concatenate([near_parts[k][way] for k in range(2)]) for way in range(2)]
        else:
            going = both_ways(going)
        held += going
        tables += [((0, 1), whose(-step)), ((0, 1), whose(step))]
        if step == 1:
            out = blank_tiles(shape, blocks[: owned // 2], going)
        if step == max(full_steps - 1, 1):
            out = blank_tiles(shape, blocks[owned // 2 :], going, out)
    if out is None:
        out = blank_tiles(shape, blocks, [])
    if full_steps:
        first = both_ways([own[0], own[0]])
        going, first = lax.optimization_barrier((going, first))
    if split:
        held += both_ways([going[0][:owned], going[1][owned:]])
        tables += [((0,), whose(full_steps + 1)), ((1,), whose(full_steps + 1))]
    own.append(compact(got, capacity, width, counts[0], counts[1], note_rows))
    settled, _ = lax.optimization_barrier((own, going))
    near, pick = settle_own(settled, owned, sizes)

    streams = [[own[half], own[half]] for half in range(2)]
    arrived = []
    weights = None

    def advance(out, weights):
        if weights is None:
            x_full, z_full, out = first_tiles(held, own, (near, pick), out, tables, sizes)
            return out, (x_full, z_full, near, pick)
        pieces, noted, spans = arrived.pop(0)
        return next_tiles(pieces, noted, spans, weights, out, sizes), weights

    sends = [(step, half) for step in range(1, full_steps + 1 + split) for half in range(2)]
    done = 0
    for sent, (step, half) in enumerate(sends):
        moving = streams[half]
        if sent == 2:
            moving, near, pick = lax.optimization_barrier((moving, near, pick))
        wanted = max(KERNELS[sent] if sent < len(KERNELS) else sent - 1, 0)
        if done < wanted:
            while done < wanted:
                out, weights = advance(out, weights)
                done += 1
            moving, out = lax.optimization_barrier((moving, out))
        if step <= full_steps:
            moving = first if sent == 0 else both_ways(moving)
            spans = [(k, note_rows, k * note_rows, counts[half]) for k in range(2)]
            arrived.append((moving, 2, spans))
            streams[half] = moving
        else:
            part = counts[half] // 2
            cut = note_rows + part * width
            moving = both_ways([moving[0][:cut], moving[1][cut:]])
            spans = [(0, note_rows, 0, part), (1, 0, part, counts[half] - part)]
            arrived.append((moving, 1, spans))
    if weights is None:
        out, weights = advance(out, weights)
    while arrived:
        out, weights = advance(out, weights)
    return out


def solution(mesh):
    placed = (
        P(("row", "col"), None, None),
        P(("row", "col"), None),
        P(("row", "col")),
        P("row", "col", None),
        P("row", "col", None),
    )
    return jax.shard_map(
        body, mesh=mesh, in_specs=placed, out_specs=P("row", None, "col"), check_vma=False
    )
```

```python
import functools
import math

import jax
import jax.numpy as jnp
from jax import lax
from jax.experimental import pallas as pl
from jax.experimental.pallas import tpu as pltpu
from jax.sharding import PartitionSpec as P

GMAX = 16
LANES = 128
VMEM_LIMIT = 32 * 1024 * 1024
UNROLL = 5
KERNELS = (0, 0, 0, 1, 2, 4, 5, 6)


def round_up(value, unit):
    return (value + unit - 1) // unit * unit


def ring_order(count):
    inner = max(d for d in range(1, math.isqrt(count) + 1) if count % d == 0)
    outer = count // inner
    path = []
    for line in range(outer):
        places = range(1, inner) if line % 2 == 0 else range(inner - 1, 0, -1)
        path += [line * inner + place for place in places]
    return path + [line * inner for line in range(outer - 1, -1, -1)]


def dot(left, right):
    return jnp.dot(left, right, preferred_element_type=jnp.float32)


def partner(place, turn, count):
    return place ^ turn if count & (count - 1) == 0 else (place + turn) % count


def side_by_side(counts):
    return max(k for k in range(1, UNROLL + 1) if all(count % k == 0 for count in counts))


def cost(groups, order, width, near, extra_bytes=0):
    steps = groups * width * order * (4 * order + 8 * near)
    moved = groups * width * (2 * order + 4 * near) + extra_bytes
    return pl.CostEstimate(flops=2 * steps, bytes_accessed=moved, transcendentals=0)


def whole(space=pltpu.VMEM):
    return pl.BlockSpec(memory_space=space)


def pack_kernel(dims, slot_ref, rows_ref, basis_ref, *refs):
    row_count, capacity, owned = dims
    outs = refs[:row_count]
    bins, notes, facts, counts, sems = refs[row_count:]
    groups, order, width = basis_ref.shape
    my_row = lax.axis_index("row")
    notes[...] = jnp.zeros_like(notes)
    facts[...] = jnp.zeros_like(facts)
    for shift in range(row_count):
        counts[shift] = 0
    lane = lax.broadcasted_iota(jnp.int32, (1, LANES), 1)

    def place(g, carry):
        slot = slot_ref[g]
        block = slot // GMAX
        owner = block // owned
        if row_count & (row_count - 1) == 0:
            shift = owner ^ my_row
        else:
            shift = lax.rem(owner - my_row + row_count, row_count)
        at = counts[shift]
        counts[shift] = at + 1
        start = pl.multiple_of(notes.shape[1] + at * width, 16)
        bins[shift, pl.ds(start, width), :] = basis_ref[g].T
        notes[shift, pl.ds(at, 1), :] = rows_ref[pl.ds(g, 1), :].astype(jnp.float32)
        fact = jnp.where(lane == 0, block - owner * owned + 1, 0)
        fact = jnp.where(lane == 1, slot - block * GMAX, fact)
        facts[shift, pl.ds(at, 1), :] = fact.astype(jnp.float32)
        return carry

    lax.fori_loop(0, groups, place, 0)
    copies = []
    for shift in range(row_count):
        bins[shift, : notes.shape[1], :width] = notes[shift].astype(jnp.bfloat16)
        bins[shift, : notes.shape[1], width : width + LANES] = facts[shift].astype(jnp.bfloat16)
        copies.append(pltpu.make_async_copy(bins.at[shift], outs[shift], sems.at[shift]))
        copies[-1].start()
    for copy in copies:
        copy.wait()


def pack(slots, rows, basis, row_count, capacity, owned):
    groups, order, width = basis.shape
    note_rows = round_up(capacity, 16)
    shape = (capacity * width + note_rows, order)
    return pl.pallas_call(
        functools.partial(pack_kernel, (row_count, capacity, owned)),
        out_shape=[jax.ShapeDtypeStruct(shape, jnp.bfloat16)] * row_count,
        in_specs=[whole(pltpu.SMEM), whole(), whole()],
        out_specs=[whole(pl.ANY)] * row_count,
        scratch_shapes=[
            pltpu.VMEM((row_count,) + shape, jnp.bfloat16),
            pltpu.VMEM((row_count, note_rows, width), jnp.float32),
            pltpu.VMEM((row_count, note_rows, LANES), jnp.float32),
            pltpu.SMEM((row_count,), jnp.int32),
            pltpu.SemaphoreType.DMA((row_count,)),
        ],
        compiler_params=pltpu.CompilerParams(vmem_limit_bytes=VMEM_LIMIT),
        name="pack",
    )(slots, rows, basis)


def compact_kernel(dims, *refs):
    capacity, width, skip, take, bin_notes, note_rows = dims
    bin_count = len(refs) - 9
    bins, out = refs[:bin_count], refs[bin_count]
    notes_in, notes, facts_in, facts, numbers, scalars, counts, sem = refs[bin_count + 1 :]
    for shift in range(bin_count):
        notes_in[shift] = bins[shift][:bin_notes, :width].astype(jnp.float32)
        facts_in[shift] = bins[shift][:bin_notes, width : width + LANES].astype(jnp.float32)
        numbers[shift] = facts_in[shift].astype(jnp.int32)
    copy = pltpu.make_async_copy(numbers, scalars, sem)
    copy.start()
    notes[...] = jnp.zeros_like(notes)
    facts[...] = jnp.zeros_like(facts)
    counts[0] = 0
    copy.wait()
    for shift in range(bin_count):
        for k in range(capacity):
            here = scalars[shift, k, 0] > 0
            seen = counts[0]
            counts[0] = seen + here.astype(jnp.int32)
            place = seen - skip

            @pl.when(here & (place >= 0) & (place < take))
            def _():
                notes[pl.ds(place, 1), :] = notes_in[shift, k : k + 1, :]
                facts[pl.ds(place, 1), :] = facts_in[shift, k : k + 1, :]
                start = pl.multiple_of(note_rows + place * width, 16)
                source = bin_notes + k * width
                out[pl.ds(start, width), :] = bins[shift][source : source + width, :]

    out[:note_rows, :width] = notes[...].astype(jnp.bfloat16)
    out[:note_rows, width : width + LANES] = facts[...].astype(jnp.bfloat16)


def compact(bins, capacity, width, skip, take, note_rows):
    bin_count = len(bins)
    order = bins[0].shape[1]
    bin_notes = bins[0].shape[0] - capacity * width
    dims = (capacity, width, skip, take, bin_notes, note_rows)
    return pl.pallas_call(
        functools.partial(compact_kernel, dims),
        out_shape=jax.ShapeDtypeStruct((note_rows + take * width, order), jnp.bfloat16),
        in_specs=[whole()] * bin_count,
        out_specs=whole(),
        scratch_shapes=[
            pltpu.VMEM((bin_count, bin_notes, width), jnp.float32),
            pltpu.VMEM((note_rows, width), jnp.float32),
            pltpu.VMEM((bin_count, bin_notes, LANES), jnp.float32),
            pltpu.VMEM((note_rows, LANES), jnp.float32),
            pltpu.VMEM((bin_count, bin_notes, LANES), jnp.int32),
            pltpu.SMEM((bin_count, bin_notes, LANES), jnp.int32),
            pltpu.SMEM((1,), jnp.int32),
            pltpu.SemaphoreType.DMA,
        ],
        compiler_params=pltpu.CompilerParams(vmem_limit_bytes=VMEM_LIMIT),
        name="compact",
    )(*bins)


def read_notes(pieces, notes, facts):
    note_rows = notes.shape[0] // len(pieces)
    width = notes.shape[1]
    for k, piece in enumerate(pieces):
        rows = slice(k * note_rows, (k + 1) * note_rows)
        notes[rows, :] = piece[:note_rows, :width].astype(jnp.float32)
        numbers = piece[:note_rows, width : width + LANES].astype(jnp.float32)
        facts[rows, :] = numbers.astype(jnp.int32)


def spot_of(facts, note):
    fact = facts[pl.ds(note, 1), :]
    return fact[0, 0] - 1, fact[0, 1]


def tiles_of(spans, width, notes, facts, weights, out, stage, stage_sems):
    x_ref, z_ref, near_ref, pick_ref = weights
    order = x_ref.shape[1]
    unroll = stage.shape[0] // 2
    lane = lax.broadcasted_iota(jnp.int32, (width, order), 1).astype(jnp.float32)
    repeats = order // width

    def send(b, p, slot):
        start = pl.multiple_of(p * width, width)
        return pltpu.make_async_copy(
            stage.at[slot], out.at[b, pl.ds(start, width), :], stage_sems.at[slot]
        )

    def images(piece, note, start):
        b, p = spot_of(facts, note)
        vectors = piece[pl.ds(start, width), :]
        turned = jnp.broadcast_to(notes[pl.ds(note, 1), :], (width, width)).T
        row_pick = (jnp.concatenate([turned] * repeats, axis=1) == lane).astype(jnp.bfloat16)
        left = jnp.concatenate([vectors, row_pick], axis=0)
        x_half = dot(left, x_ref[b]).astype(jnp.bfloat16)
        z_half = dot(left, z_ref[b]).astype(jnp.bfloat16)
        return b, p, jnp.concatenate([x_half, z_half], axis=0)

    def tile(b, p, halves, slot):
        su, se = dot(halves, near_ref[b]), dot(halves, pick_ref[b])
        su_yx, su_x, su_yz, su_z = (su[k * width : (k + 1) * width] for k in range(4))
        se_yx, se_x, se_yz, se_z = (se[k * width : (k + 1) * width] for k in range(4))
        stage[slot] = (su_x * se_yz + se_x * su_yz) + (su_yx * se_z + se_yx * su_z)
        send(b, p, slot).start()

    def side_by_side_tiles(piece, first, base, count, bank):
        found = [
            images(piece, first + k, pl.multiple_of(base + k * width, 16)) for k in range(count)
        ]
        for k, held in enumerate(found):
            tile(*held, bank * unroll + k)

    waiting = [0, 0]

    def drain(bank, count):
        for k in range(count):
            send(0, 0, bank * unroll + k).wait()

    rounds = 0
    for piece, base, first, count in spans:
        full, rest = divmod(count, unroll)
        if full > 2:
            for bank in range(2):
                drain(bank, waiting[bank])

            def body(i, carry, piece=piece, base=base, first=first):
                bank = lax.rem(i, 2)

                @pl.when(i >= 2)
                def _():
                    drain(bank, unroll)

                at = i * unroll
                side_by_side_tiles(piece, first + at, base + at * width, unroll, bank)
                return carry

            lax.fori_loop(0, full, body, 0)
            waiting[:] = [unroll, unroll]
            rounds = full
        sizes = [] if full > 2 else [unroll] * full
        done = full * unroll if full > 2 else 0
        for size in sizes + ([rest] if rest else []):
            bank = rounds % 2
            drain(bank, waiting[bank])
            side_by_side_tiles(piece, first + done, base + done * width, size, bank)
            waiting[bank] = size
            done += size
            rounds += 1
    for bank in range(2):
        drain(bank, waiting[bank])


def blank_kernel(blocks, *refs):
    out, blank, sems = refs[-3:]
    blank[...] = jnp.zeros_like(blank)
    deep_rows = blank.shape[0]
    per_block = out.shape[1] // deep_rows
    copies = []
    for b in blocks:
        for k in range(per_block):
            copies.append(
                pltpu.make_async_copy(
                    blank,
                    out.at[b, pl.ds(k * deep_rows, deep_rows), :],
                    sems.at[(b - blocks[0]) * per_block + k],
                )
            )
            copies[-1].start()
    for copy in copies:
        copy.wait()


def blank_tiles(shape, blocks, after, out=None):
    held = list(after) if out is None else [*after, out]
    deep_rows = shape[1] // 2
    return pl.pallas_call(
        functools.partial(blank_kernel, blocks),
        out_shape=jax.ShapeDtypeStruct(shape, jnp.float32),
        in_specs=[whole(pl.ANY)] * len(held),
        out_specs=whole(pl.ANY),
        input_output_aliases={} if out is None else {len(after): 0},
        scratch_shapes=[
            pltpu.VMEM((deep_rows, shape[2]), jnp.float32),
            pltpu.SemaphoreType.DMA((2 * len(blocks),)),
        ],
        cost_estimate=pl.CostEstimate(
            flops=0, bytes_accessed=4 * len(blocks) * shape[1] * shape[2], transcendentals=0
        ),
        compiler_params=pltpu.CompilerParams(vmem_limit_bytes=VMEM_LIMIT),
        name="blank_tiles",
    )(*held)


def settle_kernel(dims, *refs):
    counts, places, width, note_rows = dims
    pieces, (near_ref, pick_ref) = refs[:2], refs[2:4]
    notes, facts, near_rows = refs[4:]
    my_col = lax.axis_index("col")
    owned, order = near_ref.shape[:2]
    near_ref[...] = jnp.zeros_like(near_ref)
    near_rows[...] = jnp.full(near_rows.shape, -1.0, jnp.float32)
    read_notes(pieces, notes, facts)

    for piece, count, first in zip(pieces, counts, (0, note_rows)):

        def settle(g, carry, piece=piece, first=first):
            b, place = spot_of(facts, first + g)
            place = place - my_col * places
            start = pl.multiple_of(note_rows + g * width, 16)
            turned = piece[pl.ds(start, width), :].T
            for k in range(places):

                @pl.when(place == k)
                def _():
                    near_ref[b, :, k * width : (k + 1) * width] = turned
                    near_rows[b, k : k + 1, :] = notes[pl.ds(first + g, 1), :]

            return carry

        lax.fori_loop(0, count, settle, 0)
    deep = lax.broadcasted_iota(jnp.int32, (order, width), 0).astype(jnp.float32)

    def picks(b, carry):
        for k in range(places):
            hit = near_rows[b, k : k + 1, :] == deep
            pick_ref[b, :, k * width : (k + 1) * width] = hit.astype(jnp.bfloat16)
        return carry

    lax.fori_loop(0, owned, picks, 0)


def settle_own(pieces, owned, sizes):
    counts, places, width, note_rows = sizes
    order = pieces[0].shape[1]
    near = places * width
    narrow = jax.ShapeDtypeStruct((owned, order, near), jnp.bfloat16)
    return pl.pallas_call(
        functools.partial(settle_kernel, (counts, places, width, note_rows)),
        out_shape=[narrow, narrow],
        in_specs=[whole()] * 2,
        out_specs=[whole()] * 2,
        scratch_shapes=[
            pltpu.VMEM((2 * note_rows, width), jnp.float32),
            pltpu.VMEM((2 * note_rows, LANES), jnp.int32),
            pltpu.VMEM((owned, round_up(places, 8), width), jnp.float32),
        ],
        cost_estimate=pl.CostEstimate(
            flops=0, bytes_accessed=8 * owned * order * near, transcendentals=0
        ),
        compiler_params=pltpu.CompilerParams(vmem_limit_bytes=VMEM_LIMIT),
        name="settle_own",
    )(*pieces)


def first_kernel(dims, tables, *refs):
    counts, width, note_rows, parts, part = dims
    held = refs[:parts]
    refs = refs[parts:]
    pieces, near_ref, pick_ref, x_ref, z_ref, out = refs[:2], *refs[2:4], *refs[5:8]
    owned = x_ref.shape[0]
    notes, facts, stage, part_sems, stage_sems = refs[8:]
    my_col = lax.axis_index("col")
    copies = []
    for k, (sides, sources) in enumerate(tables):
        col = jnp.int32(0)
        for c, source in enumerate(sources):
            col = jnp.where(my_col == c, jnp.int32(source), col)
        start = pl.multiple_of(col * part, part)
        for at, side in enumerate(sides):
            copies.append(
                pltpu.make_async_copy(
                    held[k].at[pl.ds(at * owned, owned)],
                    (x_ref, z_ref)[side].at[:, pl.ds(start, part), :],
                    part_sems.at[2 * k + at],
                )
            )
            copies[-1].start()
    read_notes(pieces, notes, facts)
    for copy in copies:
        copy.wait()
    spans = [
        (piece, note_rows, first, count)
        for piece, count, first in zip(pieces, counts, (0, note_rows))
    ]
    weights = (x_ref, z_ref, near_ref, pick_ref)
    tiles_of(spans, width, notes, facts, weights, out, stage, stage_sems)


def first_tiles(held, pieces, near_weights, out, tables, sizes):
    counts, places, width, note_rows = sizes
    parts = len(held)
    owned = out.shape[0]
    part, order = held[0].shape[1:]
    near = places * width
    slots = 2 * side_by_side(counts)
    square = jax.ShapeDtypeStruct((owned, order, order), jnp.bfloat16)
    return pl.pallas_call(
        functools.partial(first_kernel, (counts, width, note_rows, parts, part), tables),
        out_shape=[square, square, jax.ShapeDtypeStruct(out.shape, out.dtype)],
        in_specs=[whole(pl.ANY)] * parts + [whole()] * 4 + [whole(pl.ANY)],
        out_specs=[whole()] * 2 + [whole(pl.ANY)],
        input_output_aliases={parts + 4: 2},
        scratch_shapes=[
            pltpu.VMEM((2 * note_rows, width), jnp.float32),
            pltpu.VMEM((2 * note_rows, LANES), jnp.int32),
            pltpu.VMEM((slots, width, near), jnp.float32),
            pltpu.SemaphoreType.DMA((2 * parts,)),
            pltpu.SemaphoreType.DMA((slots,)),
        ],
        cost_estimate=cost(sum(counts), order, width, near),
        compiler_params=pltpu.CompilerParams(vmem_limit_bytes=VMEM_LIMIT),
        name="first_tiles",
    )(*held, *pieces, *near_weights, out)


def next_kernel(spans, width, noted, count, *refs):
    pieces, weights = refs[:count], refs[count : count + 4]
    out, notes, facts, stage, stage_sems = refs[count + 5 :]
    read_notes(pieces[:noted], notes, facts)
    spans = [(pieces[k], base, first, groups) for k, base, first, groups in spans]
    tiles_of(spans, width, notes, facts, weights, out, stage, stage_sems)


def next_tiles(pieces, noted, spans, weights, out, sizes):
    counts, places, width, note_rows = sizes
    order = weights[0].shape[1]
    near = out.shape[2]
    count = len(pieces)
    slots = 2 * side_by_side([span[3] for span in spans])
    return pl.pallas_call(
        functools.partial(next_kernel, spans, width, noted, count),
        out_shape=jax.ShapeDtypeStruct(out.shape, out.dtype),
        in_specs=[whole()] * (count + 4) + [whole(pl.ANY)],
        out_specs=whole(pl.ANY),
        input_output_aliases={count + 4: 0},
        scratch_shapes=[
            pltpu.VMEM((noted * note_rows, width), jnp.float32),
            pltpu.VMEM((noted * note_rows, LANES), jnp.int32),
            pltpu.VMEM((slots, width, near), jnp.float32),
            pltpu.SemaphoreType.DMA((slots,)),
        ],
        cost_estimate=cost(sum(span[3] for span in spans), order, width, near),
        compiler_params=pltpu.CompilerParams(vmem_limit_bytes=VMEM_LIMIT),
        name="next_tiles",
    )(*pieces, *weights, out)


def body(basis, row_index, group_slot, x_blocks, zinv_blocks):
    row_count = lax.axis_size("row")
    col_count = lax.axis_size("col")
    groups, order, width = basis.shape
    owned = x_blocks.shape[0]
    places = GMAX // col_count
    capacity = (groups + row_count - 1) // row_count
    low = groups - (row_count - 2) * capacity
    early = 2 if 0 < low < groups else row_count
    low = low if early == 2 else groups // 2
    counts = (low, groups - low)
    note_rows = round_up(max(counts), 16)
    sizes = (counts, places, width, note_rows)

    ring = ring_order(col_count)
    place_of = {col: k for k, col in enumerate(ring)}
    ahead = [(ring[k], ring[(k + 1) % col_count]) for k in range(col_count)]
    behind = [(there, here) for here, there in ahead]
    full_steps = (col_count - 1) // 2
    split = col_count % 2 == 0 and col_count > 1

    def whose(offset):
        return [ring[(place_of[col] + offset) % col_count] for col in range(col_count)]

    bins = pack(group_slot, row_index, basis, row_count, capacity, owned)
    got = [bins[0]]
    for turn in range(1, row_count):
        pairs = [(k, partner(k, turn, row_count)) for k in range(row_count)]
        got.append(lax.ppermute(bins[turn], "row", pairs))
    own = [compact(got[:early], capacity, width, 0, counts[0], note_rows)]
    pairs_of = (ahead, behind)

    def both_ways(moving):
        return [lax.ppermute(moving[way], "col", pairs_of[way]) for way in range(2)]

    shape = (owned, GMAX * width, places * width)
    blocks = list(range(owned))
    held, tables = [x_blocks, zinv_blocks], [((0,), whose(0)), ((1,), whose(0))]
    going = None
    out = None
    first = None
    for step in range(1, full_steps + 1):
        if step == 2:
            going, bins = lax.optimization_barrier((going, bins))
        if step == 3:
            going, got = lax.optimization_barrier((going, got))
        if step == 1:
            near_parts = [both_ways([part, part]) for part in (x_blocks, zinv_blocks)]
            near_parts = lax.optimization_barrier(near_parts)
            going = [jnp.concatenate([near_parts[k][way] for k in range(2)]) for way in range(2)]
        else:
            going = both_ways(going)
        held += going
        tables += [((0, 1), whose(-step)), ((0, 1), whose(step))]
        if step == 1:
            out = blank_tiles(shape, blocks[: owned // 2], going)
        if step == max(full_steps - 1, 1):
            out = blank_tiles(shape, blocks[owned // 2 :], going, out)
    if out is None:
        out = blank_tiles(shape, blocks, [])
    if full_steps:
        first = both_ways([own[0], own[0]])
        going, first = lax.optimization_barrier((going, first))
    if split:
        held += both_ways([going[0][:owned], going[1][owned:]])
        tables += [((0,), whose(full_steps + 1)), ((1,), whose(full_steps + 1))]
    own.append(compact(got, capacity, width, counts[0], counts[1], note_rows))
    settled, _ = lax.optimization_barrier((own, going))
    near, pick = settle_own(settled, owned, sizes)

    streams = [[own[half], own[half]] for half in range(2)]
    arrived = []
    weights = None

    def advance(out, weights):
        if weights is None:
            x_full, z_full, out = first_tiles(held, own, (near, pick), out, tables, sizes)
            return out, (x_full, z_full, near, pick)
        pieces, noted, spans = arrived.pop(0)
        return next_tiles(pieces, noted, spans, weights, out, sizes), weights

    sends = [(step, half) for step in range(1, full_steps + 1 + split) for half in range(2)]
    done = 0
    for sent, (step, half) in enumerate(sends):
        moving = streams[half]
        if sent == 2:
            moving, near, pick = lax.optimization_barrier((moving, near, pick))
        wanted = max(KERNELS[sent] if sent < len(KERNELS) else sent - 1, 0)
        if done < wanted:
            while done < wanted:
                out, weights = advance(out, weights)
                done += 1
            moving, out = lax.optimization_barrier((moving, out))
        if step <= full_steps:
            moving = first if sent == 0 else both_ways(moving)
            spans = [(k, note_rows, k * note_rows, counts[half]) for k in range(2)]
            arrived.append((moving, 2, spans))
            streams[half] = moving
        else:
            part = counts[half] // 2
            cut = note_rows + part * width
            moving = both_ways([moving[0][:cut], moving[1][cut:]])
            spans = [(0, note_rows, 0, part), (1, 0, part, counts[half] - part)]
            arrived.append((moving, 1, spans))
    if weights is None:
        out, weights = advance(out, weights)
    while arrived:
        out, weights = advance(out, weights)
    return out


def solution(mesh):
    placed = (
        P(("row", "col"), None, None),
        P(("row", "col"), None),
        P(("row", "col")),
        P("row", "col", None),
        P("row", "col", None),
    )
    return jax.shard_map(
        body, mesh=mesh, in_specs=placed, out_specs=P("row", None, "col"), check_vma=False
    )
```
